128 devices in a mesh: freq: 8 (over x, core), rows: 16 (over y, z).
Axes of the slice: x: 4, y: 4, z: 4, core: 2. Of those that a mesh axis runs over, the one named last changes fastest.
Arguments:
- y_inter: bfloat16 [16, 2, 4096, 4096], P('freq', None, 'rows'), parts along dimension 0
- y_out: bfloat16 [16, 2, 5120, 4096], P('freq', None, 'rows'), parts along dimension 0, may hold values from -0.09375 to 0.09375
- forces: bfloat16 [4096, 128], replicated, may hold values from -6 to 6
- pairs: int32 [2048, 2], replicated, may hold values from 0 to 4095, as said below
Outputs:
- response: float32 [16, 2, 5120, 128], P('freq', None, 'rows'), parts along dimension 0
- interface_forces: float32 [16, 2, 2048, 128], P('freq', None, 'rows'), parts along dimension 0
The draws below stay inside these ranges and needn't reach their ends.
There are 8 independent parts, one for each index of `freq`. The reference program is written for one: setup_inputs(seed, part) draws one part's arguments, and reference() takes and returns one part's arrays. A program takes and returns all parts, laid end to end along the dimension named above; an argument that names none is the same for every part. Nothing has to cross between parts.
Inputs may be any that keep to these rules, and one draw needn't show every extreme that they name: Each of the 4096 uncoupled interface degrees of freedom appears exactly once in pairs, so every index of rows holds exactly 256 of them in constraints of its own block of 128. Of the degrees of freedom s * 256 to (s + 1) * 256 - 1, at most 31 appear in the constraints d * 128 to (d + 1) * 128 - 1 for any s and d, and every s reaches 31 for one d.
All inputs are finite; a program needn't handle non-finite values.
Results may differ from the reference program's by a relative error of at most 0.0085.
Values may be sent and summed in bfloat16 or wider, within the bound.
A program may use at most 128 MiB of HBM per device.

```python
import math
import jax
import jax.numpy as jnp
from jax import lax

NI = 2048
NFQ = 2
NLOAD = 128
ITERS = 4
NB = 4096
RB = 256
NOUT = 5120


def draw_y_inter(key, part):
    key_off, key_real, key_imag = jax.random.split(jax.random.fold_in(key, 11), 3)
    spread_off = 0.6 / math.sqrt(NB)
    shape = (NFQ, 2, NB, NB)
    off_part = jax.random.truncated_normal(key_off, -4.0, 4.0, shape, jnp.float32) * spread_off
    real_diag = jax.random.uniform(key_real, (NFQ, NB), jnp.float32, 1.5, 2.5)
    imag_diag = jax.random.uniform(key_imag, (NFQ, NB), jnp.float32, 0.1, 0.6)
    identity = (jnp.arange(NB)[:, None] == jnp.arange(NB)[None, :]).astype(jnp.float32)
    diagonal = jnp.stack([real_diag, imag_diag], 1)
    return (off_part + identity[None, None] * diagonal[:, :, None, :]).astype(jnp.bfloat16)


def draw_pairs(key, part):
    key_local, key_extra, key_order = jax.random.split(jax.random.fold_in(key, 23), 3)
    devices = NB // RB
    spread_count = RB // devices - 1
    local_keys = jax.random.split(key_local, devices)
    local_perm = jax.vmap(lambda single: jax.random.permutation(single, RB))(local_keys)
    extra_target = jax.random.permutation(key_extra, devices)
    position = jnp.arange(RB, dtype=jnp.int32)
    labels = jnp.where(position[None, :] < devices * spread_count, position[None, :] // max(spread_count, 1), extra_target[:, None])
    owners = (jnp.arange(devices, dtype=jnp.int32)[:, None] * RB + local_perm).reshape(-1)
    target = jnp.zeros((NB,), jnp.int32).at[owners].set(labels.reshape(-1).astype(jnp.int32))
    shuffle = jax.random.permutation(key_order, NB).astype(jnp.int32)
    score = target * NB + shuffle
    ordering = jnp.argsort(score)
    return ordering.reshape(NI, 2).astype(jnp.int32)


def levels(stream_key, dims, shards, least, largest):
    level, own = 1.0, jax.random.fold_in(stream_key, 6)
    for dim, blocks in shards:
        heights = jnp.exp(jax.random.uniform(jax.random.fold_in(own, dim), (blocks,), jnp.float32, least / len(shards), largest / len(shards)))
        level = level * jnp.repeat(heights, dims[dim] // blocks).reshape([-1 if axis == dim else 1 for axis in range(len(dims))])
    return level


def gaussian(rng, dims, scale, bound, shards=(), kind=jnp.bfloat16):
    result = jax.random.normal(rng, dims, jnp.float32) * scale
    if len(shards) > 0:
        result = levels(rng, dims, shards, -0.22, 0.18) * result
    return jnp.clip(result, min=-bound, max=bound).astype(kind)


def setup_inputs(seed: int = 0, part: int = 0) -> dict:
    arg_keys = jax.random.split(jax.random.key(seed), 5)
    part_splits = jax.random.split(jax.random.fold_in(arg_keys[4], part), 5)
    return {
        "y_inter": draw_y_inter(jax.random.fold_in(jax.random.fold_in(arg_keys[4], part), 71), part),
        "y_out": gaussian(part_splits[1], (NFQ, 2, NOUT, NB), NB ** -0.5, 0.09375, ((2, 16),)),
        "forces": gaussian(arg_keys[2], (NB, NLOAD), 1.0, 6.0),
        "pairs": draw_pairs(jax.random.fold_in(arg_keys[4], 71), part),
    }


def complex_apply(pivot_real, pivot_imag, values):
    denom = pivot_real * pivot_real + pivot_imag * pivot_imag
    real_part = values[:, 0]
    imag_part = values[:, 1]
    first = (pivot_real[..., None] * real_part + pivot_imag[..., None] * imag_part) / denom[..., None]
    second = (pivot_real[..., None] * imag_part - pivot_imag[..., None] * real_part) / denom[..., None]
    return jnp.stack([first, second], 1)


def solver_dot(left, right):
    return jnp.einsum("fkn,fnl->fkl", left.astype(jnp.float32), right.astype(jnp.float32), precision=lax.Precision.HIGHEST)


def reference(y_inter, y_out, forces, pairs):
    plus_dof = pairs[:, 0].astype(jnp.int32)
    minus_dof = pairs[:, 1].astype(jnp.int32)
    motion = jnp.einsum("fcjn,nl->fcjl", y_inter.astype(jnp.float32), forces.astype(jnp.float32), precision=lax.Precision.HIGHEST).astype(jnp.bfloat16)
    coupled = (jnp.take(y_inter, plus_dof, axis=3).astype(jnp.float32) - jnp.take(y_inter, minus_dof, axis=3).astype(jnp.float32)).astype(jnp.bfloat16)
    system = jnp.take(coupled, plus_dof, axis=2).astype(jnp.float32) - jnp.take(coupled, minus_dof, axis=2).astype(jnp.float32)
    gap = jnp.take(motion, plus_dof, axis=2).astype(jnp.float32) - jnp.take(motion, minus_dof, axis=2).astype(jnp.float32)
    diag_index = jnp.arange(NI, dtype=jnp.int32)
    pivots = system[:, :, diag_index, diag_index]
    pivot_real = pivots[:, 0]
    pivot_imag = pivots[:, 1]
    estimate = complex_apply(pivot_real, pivot_imag, gap)
    for sweep_count in range(ITERS - 1):
        real_prod = solver_dot(system[:, 0], estimate[:, 0]) - solver_dot(system[:, 1], estimate[:, 1])
        imag_prod = solver_dot(system[:, 0], estimate[:, 1]) + solver_dot(system[:, 1], estimate[:, 0])
        product = jnp.stack([real_prod, imag_prod], 1)
        estimate = estimate + complex_apply(pivot_real, pivot_imag, gap - product)
    rounded = estimate.astype(jnp.bfloat16)
    spread = jnp.zeros((NFQ, 2, NB, NLOAD), jnp.bfloat16).at[:, :, plus_dof, :].set(rounded).at[:, :, minus_dof, :].set(-rounded)
    uncoupled = jnp.einsum("fcrn,nl->fcrl", y_out.astype(jnp.float32), forces.astype(jnp.float32), precision=lax.Precision.HIGHEST)
    real_corr = solver_dot(y_out[:, 0], spread[:, 0]) - solver_dot(y_out[:, 1], spread[:, 1])
    imag_corr = solver_dot(y_out[:, 0], spread[:, 1]) + solver_dot(y_out[:, 1], spread[:, 0])
    correction = jnp.stack([real_corr, imag_corr], 1)
    return (uncoupled - correction, estimate)
```

```python
import functools

import jax
import jax.numpy as jnp
from jax import lax
from jax.experimental import pallas as pl
from jax.experimental.pallas import tpu as pltpu
from jax.sharding import PartitionSpec as P

ITERS = 4
SIDE = 4
SLOTS = 32
WIDE = 256
BF16 = jnp.bfloat16
F32 = jnp.float32
MESH = pl.DeviceIdType.MESH
NEAR_FIRST = (1, 3, 2)


def dot(left, right):
    return jnp.dot(left, right, preferred_element_type=F32)


def iota(shape, dim):
    return lax.broadcasted_iota(jnp.int32, shape, dim)


def total(values, axis):
    return jnp.sum(values.astype(F32), axis=axis, keepdims=True).astype(jnp.int32)


def as_column(row):
    size = row.shape[1]
    eye = iota((size, size), 0) == iota((size, size), 1)
    return total(jnp.where(eye, row, 0), 1)


def as_row(column):
    size = column.shape[0]
    eye = iota((size, size), 0) == iota((size, size), 1)
    return total(jnp.where(eye, column, 0), 0)


def kernel(
    yi_hbm, yo_hbm, fo_hbm, pt, resp, lam,
    yi, yo, fo, e, c, co, g, sbuf, rbuf, dsend, drecv, gap, piv, pack, unpack, place, partner, delta,
    load_sem, a2a_send, a2a_recv, d_send, d_recv, g_send, p1_recv, p2_recv,
):
    devices = SIDE * SIDE
    me = lax.axis_index("rows")
    group = lax.axis_index("freq")
    my, mz = me // SIDE, me % SIDE
    nfreq, _, rows, width = yi.shape
    outs = yo.shape[2]
    cons = unpack.shape[0]
    loads = fo.shape[1]
    blocks = 2 * cons * devices // 2 // WIDE

    barrier = pltpu.get_barrier_semaphore()

    def greet(i, carry):
        pl.semaphore_signal(barrier, inc=1, device_id=(group, (me + i) % devices), device_id_type=MESH)
        return carry

    lax.fori_loop(1, devices, greet, 0)

    load_fo = pltpu.make_async_copy(fo_hbm, fo, load_sem.at[0])
    load_yi = [[pltpu.make_async_copy(yi_hbm.at[f, k], yi.at[f, k], load_sem.at[1 + 2 * f + k]) for k in range(2)] for f in range(nfreq)]
    load_yo = [pltpu.make_async_copy(yo_hbm.at[f], yo.at[f], load_sem.at[5 + f]) for f in range(nfreq)]
    load_fo.start()
    for f in range(nfreq):
        for k in range(2):
            load_yi[f][k].start()
    for f in range(nfreq):
        load_yo[f].start()

    step = 32

    def find(b, carry):
        first = pl.multiple_of(b * step, step)
        wide = (step, pt.shape[1])
        dof = iota(wide, 0) + (me * rows + first)
        plus, minus = pt[0:1, :], pt[1:2, :]
        is_plus, is_minus = plus == dof, minus == dof
        index = 2 * iota(wide, 1)
        place[pl.ds(first, step), :] = total(jnp.where(is_plus, index, jnp.where(is_minus, index + 1, 0)), 1)
        partner[pl.ds(first, step), :] = total(jnp.where(is_plus, minus, jnp.where(is_minus, plus, 0)), 1)
        return carry

    lax.fori_loop(0, rows // step, find, 0)
    place_col = place[...]
    place_row = as_row(place_col)
    goal_col, goal_row = place_col // (2 * cons), place_row // (2 * cons)
    rank_row = total(jnp.where((goal_col == goal_row) & (place_col < place_row), 1, 0), 0)
    slot_row = goal_row * SLOTS + rank_row
    pack[...] = jnp.where(iota(pack.shape, 0) == slot_row, 1.0, 0.0).astype(BF16)

    mine = pl.ds(pl.multiple_of(me * cons, cons), cons)
    plus_row, minus_row = pt[0:1, mine], pt[1:2, mine]
    from_plus_row, from_minus_row = plus_row // rows, minus_row // rows
    from_plus_col, from_minus_col = as_column(plus_row) // rows, as_column(minus_row) // rows
    square = (cons, cons)
    before = iota(square, 1) < iota(square, 0)
    upto = iota(square, 1) <= iota(square, 0)
    rank_plus = total(jnp.where(before & (from_plus_row == from_plus_col), 1, 0) + jnp.where(before & (from_minus_row == from_plus_col), 1, 0), 1)
    rank_minus = total(jnp.where(before & (from_minus_row == from_minus_col), 1, 0) + jnp.where(upto & (from_plus_row == from_minus_col), 1, 0), 1)
    spot = iota(unpack.shape, 1)
    at_plus = spot == from_plus_col * SLOTS + rank_plus
    at_minus = spot == from_minus_col * SLOTS + rank_minus
    unpack[...] = jnp.where(at_plus, 1.0, jnp.where(at_minus, -1.0, 0.0)).astype(BF16)

    def exchange(send, recv, send_sem, recv_sem):
        def one(i, carry):
            peer = (me + i) % devices
            pltpu.make_async_remote_copy(
                src_ref=send.at[peer], dst_ref=recv.at[me], send_sem=send_sem, recv_sem=recv_sem,
                device_id=(group, peer), device_id_type=MESH,
            ).start()
            return carry

        lax.fori_loop(1, devices, one, 0)

    def wait_bytes(ref, sem):
        pltpu.make_async_copy(ref, ref, sem).wait()

    def send_rows(f, values):
        packed = dot(pack[...], values.astype(BF16)).astype(BF16).reshape(devices, SLOTS, 2 * loads)
        sbuf[f] = packed
        rbuf[f, me] = sbuf[f, me]
        exchange(sbuf.at[f], rbuf.at[f], a2a_send.at[f], a2a_recv.at[f])

    def side_by_side(f):
        return jnp.concatenate([dot(yi[f, 0], fo[...]), dot(yi[f, 1], fo[...])], axis=1)

    load_fo.wait()
    for f in range(nfreq):
        load_yi[f][0].wait()
        load_yi[f][1].wait()
        moved = side_by_side(f)
        if f == 0:
            pl.semaphore_wait(barrier, devices - 1)
        send_rows(f, moved)

    lane = 128

    def entries(b, carry):
        first = pl.multiple_of(b * step, step)
        here = pl.ds(first, step)
        small = (step, lane)
        own = iota(small, 0) + (me * rows + first)
        other = partner[here, :]
        sums = [jnp.zeros(small, F32) for _ in range(2 * nfreq)]
        for j in range(width // lane):
            column = iota(small, 1) + j * lane
            sign = jnp.where(column == own, 1.0, jnp.where(column == other, -1.0, 0.0))
            for q in range(2 * nfreq):
                sums[q] = sums[q] + yi[q // 2, q % 2, here, j * lane : (j + 1) * lane].astype(F32) * sign
        spread_out = jnp.zeros(small, F32)
        for q in range(2 * nfreq):
            spread_out = jnp.where(iota(small, 1) == q, jnp.sum(sums[q], axis=1, keepdims=True), spread_out)
        delta[here, :] = spread_out.astype(BF16)
        return carry

    lax.fori_loop(0, rows // step, entries, 0)
    dsend[...] = dot(pack[...], delta[...]).astype(BF16).reshape(devices, SLOTS, lane)
    drecv[me] = dsend[me]
    exchange(dsend, drecv, d_send, d_recv)

    def make_signs(kb):
        here = pl.ds(pl.multiple_of(kb * WIDE, WIDE), WIDE)

        def part(s, carry):
            first = pl.multiple_of(s * WIDE, WIDE)
            dof = iota((WIDE, WIDE), 0) + first
            e[kb, pl.ds(first, WIDE), :] = jnp.where(dof == pt[0:1, here], 1.0, jnp.where(dof == pt[1:2, here], -1.0, 0.0)).astype(BF16)
            return carry

        lax.fori_loop(0, width // WIDE, part, 0)

    def make_coupled(f, kb):
        here = pl.ds(pl.multiple_of(kb * WIDE, WIDE), WIDE)
        own = place[...] // 2
        for k in range(2):
            product = dot(yi[f, k], e[kb])
            kept = jnp.where(iota((rows, WIDE), 1) + kb * WIDE == own, 0.0, product)
            c[f, k * rows : (k + 1) * rows, here] = kept.astype(BF16)

    def make_out(f, kb):
        here = pl.ds(pl.multiple_of(kb * WIDE, WIDE), WIDE)
        for k in range(2):
            co[f, k * outs : (k + 1) * outs, here] = dot(yo[f, k], e[kb]).astype(BF16)

    def ring(steps_y, steps_z):
        return (group, ((my + steps_y) % SIDE) * SIDE + (mz + steps_z) % SIDE)

    def first_leg(f, h, d):
        ref = g.at[f, my, mz, h]
        return pltpu.make_async_remote_copy(
            src_ref=ref, dst_ref=ref, send_sem=g_send.at[f], recv_sem=p1_recv.at[f, h, d - 1],
            device_id=ring(d, 0) if h == 0 else ring(0, d), device_id_type=MESH,
        )

    def second_leg(f, h, d, far):
        ref = g.at[f, (my + SIDE - d) % SIDE, mz, h] if h == 0 else g.at[f, my, (mz + SIDE - d) % SIDE, h]
        return pltpu.make_async_remote_copy(
            src_ref=ref, dst_ref=ref, send_sem=g_send.at[f], recv_sem=p2_recv.at[f],
            device_id=ring(0, far) if h == 0 else ring(far, 0), device_id_type=MESH,
        )

    def solve_and_share(f, sweep):
        wait_bytes(rbuf.at[f, 0 : devices - 1], a2a_recv.at[f])
        arrived = dot(unpack[...], rbuf[f].reshape(devices * SLOTS, 2 * loads))
        if sweep == 0:
            if f == 0:
                wait_bytes(drecv.at[0 : devices - 1], d_recv)
                both = jnp.abs(unpack[...].astype(F32)).astype(BF16)
                piv[...] = dot(both, drecv[...].reshape(devices * SLOTS, lane))
            gap[f] = arrived
            rest = arrived
        else:
            rest = gap[f] - arrived
        pr, pi = piv[:, 2 * f : 2 * f + 1], piv[:, 2 * f + 1 : 2 * f + 2]
        denom = pr * pr + pi * pi
        xr, xi = rest[:, :loads], rest[:, loads:]
        real = (pr * xr + pi * xi) / denom
        imag = (pr * xi - pi * xr) / denom
        if sweep == ITERS - 1:
            lam[f, 0] = real
            lam[f, 1] = imag
        g[f, my, mz] = jnp.concatenate([real, imag], axis=1).astype(BF16).reshape(2, cons // 2, 2 * loads)
        for d in NEAR_FIRST:
            for h in range(2):
                first_leg(f, h, d).start()
        for far in NEAR_FIRST:
            for h in range(2):
                second_leg(f, h, 0, far).start()

    def pass_on(f):
        for d in NEAR_FIRST:
            for h in range(2):
                first_leg(f, h, d).wait_recv()
                for far in NEAR_FIRST:
                    second_leg(f, h, d, far).start()

    def gathered(f):
        wait_bytes(g.at[f, 0:3], p2_recv.at[f])
        wait_bytes(g.at[f, 0:3], g_send.at[f])
        wait_bytes(g.at[f, 0:3, 0:1], g_send.at[f])
        return g[f].reshape(cons * devices, 2 * loads)

    def complex_parts(products, count):
        top, low = products[:count], products[count:]
        return top[:, :loads] - low[:, loads:], top[:, loads:] + low[:, :loads]

    def multiply(f):
        real, imag = complex_parts(dot(c[f], gathered(f)), rows)
        wait_bytes(sbuf.at[f, 0 : devices - 1], a2a_send.at[f])
        send_rows(f, jnp.concatenate([real, imag], axis=1))

    def finish(f):
        real, imag = complex_parts(dot(co[f], gathered(f)), outs)
        resp[f, 0] = resp[f, 0] - real
        resp[f, 1] = resp[f, 1] - imag

    def span(fn, low, high):
        def one(i, carry):
            fn(i)
            return carry

        lax.fori_loop(low, high, one, 0)

    def signs_and_coupled(kb):
        make_signs(kb)
        make_coupled(0, kb)

    def out_chunk(i):
        make_out(i // blocks, i % blocks)

    span(signs_and_coupled, 0, 2)
    solve_and_share(0, 0)
    span(signs_and_coupled, 2, 4)
    pass_on(0)
    span(signs_and_coupled, 4, 6)
    solve_and_share(1, 0)
    span(signs_and_coupled, 6, 8)
    multiply(0)
    pass_on(1)
    span(functools.partial(make_coupled, 1), 0, 6)
    for f in range(nfreq):
        load_yo[f].wait()
    done = 0
    for sweep in range(1, ITERS):
        solve_and_share(0, sweep)
        if sweep == 1:
            span(functools.partial(make_coupled, 1), 6, 8)
        multiply(1)
        pass_on(0)
        more = 3 if sweep < ITERS - 1 else 2
        span(out_chunk, done, done + more)
        done += more
        solve_and_share(1, sweep)
        if sweep < ITERS - 1:
            multiply(0)
        else:
            finish(0)
        pass_on(1)
        if sweep < ITERS - 1:
            for k in range(2):
                f = sweep - 1
                resp[f, k] = dot(yo[f, k], fo[...])
            span(out_chunk, done, done + 4)
            done += 4
    finish(1)
    for f in range(nfreq):
        wait_bytes(sbuf.at[f, 0 : devices - 1], a2a_send.at[f])
    wait_bytes(dsend.at[0 : devices - 1], d_send)


def on_device(y_inter, y_out, forces, pairs):
    nfreq, _, rows, width = y_inter.shape
    outs = y_out.shape[2]
    loads = forces.shape[1]
    devices = SIDE * SIDE
    cons = pairs.shape[0] // devices
    half = cons // 2
    dma = pltpu.SemaphoreType.DMA
    hbm = pl.BlockSpec(memory_space=pl.ANY)
    vmem = pl.BlockSpec(memory_space=pltpu.VMEM)
    return pl.pallas_call(
        kernel,
        out_shape=(
            jax.ShapeDtypeStruct((nfreq, 2, outs, loads), F32),
            jax.ShapeDtypeStruct((nfreq, 2, cons, loads), F32),
        ),
        in_specs=[hbm, hbm, hbm, vmem],
        out_specs=(vmem, vmem),
        scratch_shapes=[
            pltpu.VMEM(y_inter.shape, BF16),
            pltpu.VMEM(y_out.shape, BF16),
            pltpu.VMEM(forces.shape, BF16),
            pltpu.VMEM((pairs.shape[0] // WIDE, width, WIDE), BF16),
            pltpu.VMEM((nfreq, 2 * rows, pairs.shape[0]), BF16),
            pltpu.VMEM((nfreq, 2 * outs, pairs.shape[0]), BF16),
            pltpu.VMEM((nfreq, SIDE, SIDE, 2, half, 2 * loads), BF16),
            pltpu.VMEM((nfreq, devices, SLOTS, 2 * loads), BF16),
            pltpu.VMEM((nfreq, devices, SLOTS, 2 * loads), BF16),
            pltpu.VMEM((devices, SLOTS, 128), BF16),
            pltpu.VMEM((devices, SLOTS, 128), BF16),
            pltpu.VMEM((nfreq, cons, 2 * loads), F32),
            pltpu.VMEM((cons, 128), F32),
            pltpu.VMEM((devices * SLOTS, rows), BF16),
            pltpu.VMEM((cons, devices * SLOTS), BF16),
            pltpu.VMEM((rows, 1), jnp.int32),
            pltpu.VMEM((rows, 1), jnp.int32),
            pltpu.VMEM((rows, 128), BF16),
            dma((1 + 2 * nfreq + nfreq,)),
            dma((nfreq,)),
            dma((nfreq,)),
            dma,
            dma,
            dma((nfreq,)),
            dma((nfreq, 2, SIDE - 1)),
            dma((nfreq,)),
        ],
        compiler_params=pltpu.CompilerParams(collective_id=0, has_side_effects=True, vmem_limit_bytes=60 * 2**20),
    )(y_inter, y_out, forces, pairs.T)


def solution(mesh):
    placed = P("freq", None, "rows", None)
    return jax.shard_map(
        on_device,
        mesh=mesh,
        in_specs=(placed, placed, P(), P()),
        out_specs=(placed, placed),
        check_vma=False,
    )
```

```python
import functools

import jax
import jax.numpy as jnp
from jax import lax
from jax.experimental import pallas as pl
from jax.experimental.pallas import tpu as pltpu
from jax.sharding import PartitionSpec as P

ITERS = 4
SIDE = 4
SLOTS = 32
WIDE = 256
BF16 = jnp.bfloat16
F32 = jnp.float32
MESH = pl.DeviceIdType.MESH
NEAR_FIRST = (1, 3, 2)
SIDES = (1, 3)
FORWARDED = ()


def dot(left, right):
    return jnp.dot(left, right, preferred_element_type=F32)


def iota(shape, dim):
    return lax.broadcasted_iota(jnp.int32, shape, dim)


def total(values, axis):
    return jnp.sum(values.astype(F32), axis=axis, keepdims=True).astype(jnp.int32)


def as_column(row):
    size = row.shape[1]
    eye = iota((size, size), 0) == iota((size, size), 1)
    return total(jnp.where(eye, row, 0), 1)


def as_row(column):
    size = column.shape[0]
    eye = iota((size, size), 0) == iota((size, size), 1)
    return total(jnp.where(eye, column, 0), 0)


def kernel(
    yi_hbm, yo_hbm, fo_hbm, pt, resp, lam,
    yi, yo, fo, e, c, co, g, sbuf, rbuf, dsend, drecv, gap, piv, pack, unpack, place, partner, delta,
    load_sem, a2a_send, a2a_recv, d_send, d_recv, g_send, first_recv, near_recv, far_recv,
):
    devices = SIDE * SIDE
    me = lax.axis_index("rows")
    group = lax.axis_index("freq")
    my, mz = me // SIDE, me % SIDE
    nfreq, _, rows, width = yi.shape
    outs = yo.shape[2]
    cons = unpack.shape[0]
    loads = fo.shape[1]
    blocks = cons * devices // WIDE

    barrier = pltpu.get_barrier_semaphore()

    def greet(i, carry):
        pl.semaphore_signal(barrier, inc=1, device_id=(group, (me + i) % devices), device_id_type=MESH)
        return carry

    lax.fori_loop(1, devices, greet, 0)

    load_fo = pltpu.make_async_copy(fo_hbm, fo, load_sem.at[0])
    load_yi = [[pltpu.make_async_copy(yi_hbm.at[f, k], yi.at[f, k], load_sem.at[1 + 2 * f + k]) for k in range(2)] for f in range(nfreq)]
    load_yo = [pltpu.make_async_copy(yo_hbm.at[f], yo.at[f], load_sem.at[5 + f]) for f in range(nfreq)]
    load_fo.start()
    for f in range(nfreq):
        for k in range(2):
            load_yi[f][k].start()

    step = 32

    def find(b, carry):
        first = pl.multiple_of(b * step, step)
        wide = (step, pt.shape[1])
        dof = iota(wide, 0) + (me * rows + first)
        plus, minus = pt[0:1, :], pt[1:2, :]
        is_plus, is_minus = plus == dof, minus == dof
        index = 2 * iota(wide, 1)
        place[pl.ds(first, step), :] = total(jnp.where(is_plus, index, jnp.where(is_minus, index + 1, 0)), 1)
        partner[pl.ds(first, step), :] = total(jnp.where(is_plus, minus, jnp.where(is_minus, plus, 0)), 1)
        return carry

    lax.fori_loop(0, rows // step, find, 0)
    place_col = place[...]
    place_row = as_row(place_col)
    goal_col, goal_row = place_col // (2 * cons), place_row // (2 * cons)
    rank_row = total(jnp.where((goal_col == goal_row) & (place_col < place_row), 1, 0), 0)
    slot_row = goal_row * SLOTS + rank_row
    pack[...] = jnp.where(iota(pack.shape, 0) == slot_row, 1.0, 0.0).astype(BF16)

    mine = pl.ds(pl.multiple_of(me * cons, cons), cons)
    plus_row, minus_row = pt[0:1, mine], pt[1:2, mine]
    from_plus_row, from_minus_row = plus_row // rows, minus_row // rows
    from_plus_col, from_minus_col = as_column(plus_row) // rows, as_column(minus_row) // rows
    square = (cons, cons)
    before = iota(square, 1) < iota(square, 0)
    upto = iota(square, 1) <= iota(square, 0)
    rank_plus = total(jnp.where(before & (from_plus_row == from_plus_col), 1, 0) + jnp.where(before & (from_minus_row == from_plus_col), 1, 0), 1)
    rank_minus = total(jnp.where(before & (from_minus_row == from_minus_col), 1, 0) + jnp.where(upto & (from_plus_row == from_minus_col), 1, 0), 1)
    spot = iota(unpack.shape, 1)
    at_plus = spot == from_plus_col * SLOTS + rank_plus
    at_minus = spot == from_minus_col * SLOTS + rank_minus
    unpack[...] = jnp.where(at_plus, 1.0, jnp.where(at_minus, -1.0, 0.0)).astype(BF16)

    def exchange(send, recv, send_sem, recv_sem):
        def one(i, carry):
            peer = (me + i) % devices
            pltpu.make_async_remote_copy(
                src_ref=send.at[peer], dst_ref=recv.at[me], send_sem=send_sem, recv_sem=recv_sem,
                device_id=(group, peer), device_id_type=MESH,
            ).start()
            return carry

        lax.fori_loop(1, devices, one, 0)

    def wait_bytes(ref, sem):
        pltpu.make_async_copy(ref, ref, sem).wait()

    def send_rows(f, values):
        packed = dot(pack[...], values.astype(BF16)).astype(BF16).reshape(devices, SLOTS, 2 * loads)
        sbuf[f] = packed
        rbuf[f, me] = sbuf[f, me]
        exchange(sbuf.at[f], rbuf.at[f], a2a_send.at[f], a2a_recv.at[f])

    def side_by_side(f):
        return jnp.concatenate([dot(yi[f, 0], fo[...]), dot(yi[f, 1], fo[...])], axis=1)

    def send_motion(f):
        if f == 0:
            load_fo.wait()
            load_yi[0][0].wait()
            load_yi[0][1].wait()
        moved = side_by_side(f)
        if f == 0:
            pl.semaphore_wait(barrier, devices - 1)
        send_rows(f, moved)

    send_motion(0)
    for f in range(1, nfreq):
        load_yi[f][0].wait()
        load_yi[f][1].wait()
    for f in range(nfreq):
        load_yo[f].start()

    lane = 128

    def entries(b, carry):
        first = pl.multiple_of(b * step, step)
        here = pl.ds(first, step)
        small = (step, lane)
        own = iota(small, 0) + (me * rows + first)
        other = partner[here, :]
        sums = [jnp.zeros(small, BF16) for _ in range(2 * nfreq)]
        for j in range(width // lane):
            column = iota(small, 1) + j * lane
            sign = jnp.where(column == own, 1.0, jnp.where(column == other, -1.0, 0.0)).astype(BF16)
            for q in range(2 * nfreq):
                sums[q] = sums[q] + yi[q // 2, q % 2, here, j * lane : (j + 1) * lane] * sign
        spread_out = jnp.zeros(small, F32)
        for q in range(2 * nfreq):
            spread_out = jnp.where(iota(small, 1) == q, jnp.sum(sums[q].astype(F32), axis=1, keepdims=True), spread_out)
        delta[here, :] = spread_out.astype(BF16)
        return carry

    lax.fori_loop(0, rows // step, entries, 0)
    dsend[...] = dot(pack[...], delta[...]).astype(BF16).reshape(devices, SLOTS, lane)
    drecv[me] = dsend[me]
    exchange(dsend, drecv, d_send, d_recv)
    for f in range(1, nfreq):
        send_motion(f)

    def make_signs(kb):
        here = pl.ds(pl.multiple_of(kb * WIDE, WIDE), WIDE)

        local = iota((WIDE, WIDE), 0).astype(F32).astype(BF16)
        plus, minus = pt[0:1, here], pt[1:2, here]
        none, one = jnp.zeros((WIDE, WIDE), BF16), jnp.ones((WIDE, WIDE), BF16)

        def within(index, first):
            at = index - first
            return jnp.where((at >= 0) & (at < WIDE), at, -1).astype(F32).astype(BF16)

        def part(s, carry):
            first = pl.multiple_of(s * WIDE, WIDE)
            e[kb, pl.ds(first, WIDE), :] = jnp.where(local == within(plus, first), one, jnp.where(local == within(minus, first), -one, none))
            return carry

        lax.fori_loop(0, width // WIDE, part, 0)

    def make_coupled(f, kb):
        here = pl.ds(pl.multiple_of(kb * WIDE, WIDE), WIDE)
        own = place[...] // 2
        for k in range(2):
            product = dot(yi[f, k], e[kb])
            kept = jnp.where(iota((rows, WIDE), 1) + kb * WIDE == own, 0.0, product)
            c[f, k * rows : (k + 1) * rows, here] = kept.astype(BF16)

    def make_out(f, kb):
        here = pl.ds(pl.multiple_of(kb * WIDE, WIDE), WIDE)
        for k in range(2):
            co[f, k * outs : (k + 1) * outs, here] = dot(yo[f, k], e[kb]).astype(BF16)

    def ring(steps_y, steps_z):
        return (group, ((my + steps_y) % SIDE) * SIDE + (mz + steps_z) % SIDE)

    def copy_block(f, ref, recv_sem, target):
        return pltpu.make_async_remote_copy(
            src_ref=ref, dst_ref=ref, send_sem=g_send.at[f], recv_sem=recv_sem,
            device_id=target, device_id_type=MESH,
        )

    def back(at, steps):
        return (at + SIDE - steps) % SIDE

    def first_leg(f, h, d):
        return copy_block(f, g.at[f, my, mz, h], first_recv.at[f, h, d - 1], ring(d, 0) if h == 0 else ring(0, d))

    def brought(f, h, d):
        return g.at[f, back(my, d), mz, h] if h == 0 else g.at[f, my, back(mz, d), h]

    def near(f, h, d, side):
        return copy_block(f, brought(f, h, d), near_recv.at[f, h, d, side // 2], ring(0, side) if h == 0 else ring(side, 0))

    def across(f, h, d):
        return copy_block(f, brought(f, h, d), far_recv.at[f], ring(0, 2) if h == 0 else ring(2, 0))

    def onward(f, h, d, side):
        part = pl.ds((side // 2) * (cons // 4), cons // 4)
        ref = g.at[f, back(my, d), back(mz, side), h, part] if h == 0 else g.at[f, back(my, side), back(mz, d), h, part]
        return copy_block(f, ref, far_recv.at[f], ring(0, side) if h == 0 else ring(side, 0))

    def share(f, h, d):
        for side in SIDES:
            near(f, h, d, side).start()
        if d not in FORWARDED:
            across(f, h, d).start()

    def solve_and_share(f, sweep):
        wait_bytes(rbuf.at[f, 0 : devices - 1], a2a_recv.at[f])
        arrived = dot(unpack[...], rbuf[f].reshape(devices * SLOTS, 2 * loads))
        if sweep == 0:
            if f == 0:
                wait_bytes(drecv.at[0 : devices - 1], d_recv)
                both = jnp.abs(unpack[...].astype(F32)).astype(BF16)
                piv[...] = dot(both, drecv[...].reshape(devices * SLOTS, lane))
            gap[f] = arrived
            rest = arrived
        else:
            rest = gap[f] - arrived
        pr, pi = piv[:, 2 * f : 2 * f + 1], piv[:, 2 * f + 1 : 2 * f + 2]
        denom = pr * pr + pi * pi
        xr, xi = rest[:, :loads], rest[:, loads:]
        real = (pr * xr + pi * xi) / denom
        imag = (pr * xi - pi * xr) / denom
        if sweep == ITERS - 1:
            lam[f, 0] = real
            lam[f, 1] = imag
        g[f, my, mz] = jnp.concatenate([real, imag], axis=1).astype(BF16).reshape(2, cons // 2, 2 * loads)
        for d in NEAR_FIRST:
            for h in range(2):
                first_leg(f, h, d).start()
        for h in range(2):
            share(f, h, 0)

    def pass_on(f):
        for d in NEAR_FIRST:
            for h in range(2):
                first_leg(f, h, d).wait_recv()
                share(f, h, d)

    def pass_far(f):
        for d in FORWARDED:
            for h in range(2):
                for side in SIDES:
                    near(f, h, d, side).wait_recv()
                    onward(f, h, d, side).start()

    def gathered(f):
        for d in range(SIDE):
            if d not in FORWARDED:
                for h in range(2):
                    for side in SIDES:
                        near(f, h, d, side).wait_recv()
        wait_bytes(g.at[f, 0], far_recv.at[f])
        wait_bytes(g.at[f, 0:3], g_send.at[f])
        wait_bytes(g.at[f, 0:3, 0:1], g_send.at[f])
        return g[f].reshape(cons * devices, 2 * loads)

    def complex_parts(products, count):
        top, low = products[:count], products[count:]
        return top[:, :loads] - low[:, loads:], top[:, loads:] + low[:, :loads]

    def multiply(f):
        real, imag = complex_parts(dot(c[f], gathered(f)), rows)
        wait_bytes(sbuf.at[f, 0 : devices - 1], a2a_send.at[f])
        send_rows(f, jnp.concatenate([real, imag], axis=1))

    def finish(f):
        real, imag = complex_parts(dot(co[f], gathered(f)), outs)
        resp[f, 0] = resp[f, 0] - real
        resp[f, 1] = resp[f, 1] - imag

    def span(fn, low, high):
        def one(i, carry):
            fn(i)
            return carry

        lax.fori_loop(low, high, one, 0)

    def signs_and_coupled(kb):
        make_signs(kb)
        make_coupled(0, kb)

    def out_chunk(i):
        make_out(i // blocks, i % blocks)

    span(signs_and_coupled, 0, 2)
    solve_and_share(0, 0)
    span(signs_and_coupled, 2, 4)
    pass_on(0)
    pass_far(0)
    span(signs_and_coupled, 4, 6)
    solve_and_share(1, 0)
    span(signs_and_coupled, 6, 8)
    multiply(0)
    pass_on(1)
    pass_far(1)
    span(functools.partial(make_coupled, 1), 0, 6)
    for f in range(nfreq):
        load_yo[f].wait()
    done = 0
    for sweep in range(1, ITERS):
        solve_and_share(0, sweep)
        if sweep == 1:
            span(functools.partial(make_coupled, 1), 6, 8)
        multiply(1)
        pass_on(0)
        pass_far(0)
        more = 3 if sweep < ITERS - 1 else 2
        span(out_chunk, done, done + more)
        done += more
        solve_and_share(1, sweep)
        if sweep < ITERS - 1:
            multiply(0)
        else:
            finish(0)
        pass_on(1)
        pass_far(1)
        if sweep < ITERS - 1:
            for k in range(2):
                f = sweep - 1
                resp[f, k] = dot(yo[f, k], fo[...])
            span(out_chunk, done, done + 4)
            done += 4
    finish(1)
    for f in range(nfreq):
        wait_bytes(sbuf.at[f, 0 : devices - 1], a2a_send.at[f])
    wait_bytes(dsend.at[0 : devices - 1], d_send)


def hand_over(resp, lam, resp_out, lam_out):
    resp_out[...] = resp[...]
    lam_out[...] = lam[...]


def on_device(y_inter, y_out, forces, pairs):
    nfreq, _, rows, width = y_inter.shape
    outs = y_out.shape[2]
    loads = forces.shape[1]
    devices = SIDE * SIDE
    cons = pairs.shape[0] // devices
    half = cons // 2
    dma = pltpu.SemaphoreType.DMA
    hbm = pl.BlockSpec(memory_space=pl.ANY)
    vmem = pl.BlockSpec(memory_space=pltpu.VMEM)
    made = pl.pallas_call(
        kernel,
        out_shape=(
            jax.ShapeDtypeStruct((nfreq, 2, outs, loads), F32),
            jax.ShapeDtypeStruct((nfreq, 2, cons, loads), F32),
        ),
        in_specs=[hbm, hbm, hbm, vmem],
        out_specs=(vmem, vmem),
        scratch_shapes=[
            pltpu.VMEM(y_inter.shape, BF16),
            pltpu.VMEM(y_out.shape, BF16),
            pltpu.VMEM(forces.shape, BF16),
            pltpu.VMEM((pairs.shape[0] // WIDE, width, WIDE), BF16),
            pltpu.VMEM((nfreq, 2 * rows, pairs.shape[0]), BF16),
            pltpu.VMEM((nfreq, 2 * outs, pairs.shape[0]), BF16),
            pltpu.VMEM((nfreq, SIDE, SIDE, 2, half, 2 * loads), BF16),
            pltpu.VMEM((nfreq, devices, SLOTS, 2 * loads), BF16),
            pltpu.VMEM((nfreq, devices, SLOTS, 2 * loads), BF16),
            pltpu.VMEM((devices, SLOTS, 128), BF16),
            pltpu.VMEM((devices, SLOTS, 128), BF16),
            pltpu.VMEM((nfreq, cons, 2 * loads), F32),
            pltpu.VMEM((cons, 128), F32),
            pltpu.VMEM((devices * SLOTS, rows), BF16),
            pltpu.VMEM((cons, devices * SLOTS), BF16),
            pltpu.VMEM((rows, 1), jnp.int32),
            pltpu.VMEM((rows, 1), jnp.int32),
            pltpu.VMEM((rows, 128), BF16),
            dma((1 + 2 * nfreq + nfreq,)),
            dma((nfreq,)),
            dma((nfreq,)),
            dma,
            dma,
            dma((nfreq,)),
            dma((nfreq, 2, SIDE - 1)),
            dma((nfreq, 2, SIDE, 2)),
            dma((nfreq,)),
        ],
        compiler_params=pltpu.CompilerParams(collective_id=0, has_side_effects=True, vmem_limit_bytes=60 * 2**20),
    )(y_inter, y_out, forces, pairs.T)
    return pl.pallas_call(
        hand_over,
        out_shape=tuple(jax.ShapeDtypeStruct(m.shape, F32) for m in made),
        in_specs=[vmem, vmem],
        out_specs=(vmem, vmem),
    )(*made)


def solution(mesh):
    placed = P("freq", None, "rows", None)
    return jax.shard_map(
        on_device,
        mesh=mesh,
        in_specs=(placed, placed, P(), P()),
        out_specs=(placed, placed),
        check_vma=False,
    )
```

```python
import functools

import jax
import jax.numpy as jnp
from jax import lax
from jax.experimental import pallas as pl
from jax.experimental.pallas import tpu as pltpu
from jax.sharding import PartitionSpec as P

ITERS = 4
SIDE = 4
SLOTS = 32
WIDE = 256
BF16 = jnp.bfloat16
F32 = jnp.float32
MESH = pl.DeviceIdType.MESH
NEAR_FIRST = (1, 3, 2)
FAR_FIRST = (2, 1, 3)
FAR_PEERS = sorted(((y, z) for y in range(SIDE) for z in range(SIDE) if y + z > 0), key=lambda p: -min(p[0], SIDE - p[0]) - min(p[1], SIDE - p[1]))
C1 = (6, 8)
OUT = ((2, 2), (2, 2))


def dot(left, right):
    return jnp.dot(left, right, preferred_element_type=F32)


def iota(shape, dim):
    return lax.broadcasted_iota(jnp.int32, shape, dim)


def total(values, axis):
    return jnp.sum(values.astype(F32), axis=axis, keepdims=True).astype(jnp.int32)


def as_column(row):
    size = row.shape[1]
    eye = iota((size, size), 0) == iota((size, size), 1)
    return total(jnp.where(eye, row, 0), 1)


def as_row(column):
    size = column.shape[0]
    eye = iota((size, size), 0) == iota((size, size), 1)
    return total(jnp.where(eye, column, 0), 0)


def kernel(
    yi_hbm, yo_hbm, fo_hbm, pt, resp, lam,
    yi, yo, fo, e, c, co, spread, g, sbuf, rbuf, dsend, drecv, gap, piv, pack, unpack, place, partner, delta,
    load_sem, a2a_send, a2a_recv, d_send, d_recv, g_send, first_recv, second_recv,
):
    devices = SIDE * SIDE
    me = lax.axis_index("rows")
    group = lax.axis_index("freq")
    my, mz = me // SIDE, me % SIDE
    nfreq, _, rows, width = yi.shape
    outs = yo.shape[2]
    cons = unpack.shape[0]
    loads = fo.shape[1]
    blocks = cons * devices // WIDE

    barrier = pltpu.get_barrier_semaphore()

    def greet(i, carry):
        pl.semaphore_signal(barrier, inc=1, device_id=(group, (me + i) % devices), device_id_type=MESH)
        return carry

    lax.fori_loop(1, devices, greet, 0)

    load_fo = pltpu.make_async_copy(fo_hbm, fo, load_sem.at[0])
    load_yi = [[pltpu.make_async_copy(yi_hbm.at[f, k], yi.at[f, k], load_sem.at[1 + 2 * f + k]) for k in range(2)] for f in range(nfreq)]
    load_yo = [pltpu.make_async_copy(yo_hbm.at[f], yo.at[f], load_sem.at[5 + f]) for f in range(nfreq)]
    load_fo.start()
    for f in range(nfreq):
        for k in range(2):
            load_yi[f][k].start()

    step = 32

    def find(b, carry):
        first = pl.multiple_of(b * step, step)
        wide = (step, pt.shape[1])
        dof = iota(wide, 0) + (me * rows + first)
        plus, minus = pt[0:1, :], pt[1:2, :]
        is_plus, is_minus = plus == dof, minus == dof
        index = 2 * iota(wide, 1)
        place[pl.ds(first, step), :] = total(jnp.where(is_plus, index, jnp.where(is_minus, index + 1, 0)), 1)
        partner[pl.ds(first, step), :] = total(jnp.where(is_plus, minus, jnp.where(is_minus, plus, 0)), 1)
        return carry

    lax.fori_loop(0, rows // step, find, 0)
    place_col = place[...]
    place_row = as_row(place_col)
    goal_col, goal_row = place_col // (2 * cons), place_row // (2 * cons)
    rank_row = total(jnp.where((goal_col == goal_row) & (place_col < place_row), 1, 0), 0)
    slot_row = goal_row * SLOTS + rank_row
    pack[...] = jnp.where(iota(pack.shape, 0) == slot_row, 1.0, 0.0).astype(BF16)

    mine = pl.ds(pl.multiple_of(me * cons, cons), cons)
    plus_row, minus_row = pt[0:1, mine], pt[1:2, mine]
    from_plus_row, from_minus_row = plus_row // rows, minus_row // rows
    from_plus_col, from_minus_col = as_column(plus_row) // rows, as_column(minus_row) // rows
    square = (cons, cons)
    before = iota(square, 1) < iota(square, 0)
    upto = iota(square, 1) <= iota(square, 0)
    rank_plus = total(jnp.where(before & (from_plus_row == from_plus_col), 1, 0) + jnp.where(before & (from_minus_row == from_plus_col), 1, 0), 1)
    rank_minus = total(jnp.where(before & (from_minus_row == from_minus_col), 1, 0) + jnp.where(upto & (from_plus_row == from_minus_col), 1, 0), 1)
    spot = iota(unpack.shape, 1)
    at_plus = spot == from_plus_col * SLOTS + rank_plus
    at_minus = spot == from_minus_col * SLOTS + rank_minus
    unpack[...] = jnp.where(at_plus, 1.0, jnp.where(at_minus, -1.0, 0.0)).astype(BF16)

    def exchange(send, recv, send_sem, recv_sem):
        for dy, dz in FAR_PEERS:
            peer = ((my + dy) % SIDE) * SIDE + (mz + dz) % SIDE
            pltpu.make_async_remote_copy(
                src_ref=send.at[peer], dst_ref=recv.at[me], send_sem=send_sem, recv_sem=recv_sem,
                device_id=(group, peer), device_id_type=MESH,
            ).start()

    def wait_bytes(ref, sem):
        pltpu.make_async_copy(ref, ref, sem).wait()

    def send_rows(f, values):
        packed = dot(pack[...], values.astype(BF16)).astype(BF16).reshape(devices, SLOTS, 2 * loads)
        sbuf[f] = packed
        rbuf[f, me] = sbuf[f, me]
        exchange(sbuf.at[f], rbuf.at[f], a2a_send.at[f], a2a_recv.at[f])

    def side_by_side(f):
        return jnp.concatenate([dot(yi[f, 0], fo[...]), dot(yi[f, 1], fo[...])], axis=1)

    def send_motion(f):
        if f == 0:
            load_fo.wait()
            load_yi[0][0].wait()
            load_yi[0][1].wait()
        moved = side_by_side(f)
        if f == 0:
            pl.semaphore_wait(barrier, devices - 1)
        send_rows(f, moved)

    send_motion(0)
    for f in range(1, nfreq):
        load_yi[f][0].wait()
        load_yi[f][1].wait()
    for f in range(nfreq):
        load_yo[f].start()

    lane = 128

    def entries(b, carry):
        first = pl.multiple_of(b * step, step)
        here = pl.ds(first, step)
        small = (step, lane)
        own = iota(small, 0) + (me * rows + first)
        other = partner[here, :]
        sums = [jnp.zeros(small, BF16) for _ in range(2 * nfreq)]
        for j in range(width // lane):
            column = iota(small, 1) + j * lane
            sign = jnp.where(column == own, 1.0, jnp.where(column == other, -1.0, 0.0)).astype(BF16)
            for q in range(2 * nfreq):
                sums[q] = sums[q] + yi[q // 2, q % 2, here, j * lane : (j + 1) * lane] * sign
        spread_out = jnp.zeros(small, F32)
        for q in range(2 * nfreq):
            spread_out = jnp.where(iota(small, 1) == q, jnp.sum(sums[q].astype(F32), axis=1, keepdims=True), spread_out)
        delta[here, :] = spread_out.astype(BF16)
        return carry

    lax.fori_loop(0, rows // step, entries, 0)
    dsend[...] = dot(pack[...], delta[...]).astype(BF16).reshape(devices, SLOTS, lane)
    drecv[me] = dsend[me]
    exchange(dsend, drecv, d_send, d_recv)
    for f in range(1, nfreq):
        send_motion(f)

    def make_signs(kb):
        here = pl.ds(pl.multiple_of(kb * WIDE, WIDE), WIDE)

        local = iota((WIDE, WIDE), 0).astype(F32).astype(BF16)
        plus, minus = pt[0:1, here], pt[1:2, here]
        none, one = jnp.zeros((WIDE, WIDE), BF16), jnp.ones((WIDE, WIDE), BF16)

        def within(index, first):
            at = index - first
            return jnp.where((at >= 0) & (at < WIDE), at, -1).astype(F32).astype(BF16)

        def part(s, carry):
            first = pl.multiple_of(s * WIDE, WIDE)
            e[kb, pl.ds(first, WIDE), :] = jnp.where(local == within(plus, first), one, jnp.where(local == within(minus, first), -one, none))
            return carry

        lax.fori_loop(0, width // WIDE, part, 0)

    def make_coupled(f, kb):
        here = pl.ds(pl.multiple_of(kb * WIDE, WIDE), WIDE)
        own = place[...] // 2
        for k in range(2):
            product = dot(yi[f, k], e[kb])
            kept = jnp.where(iota((rows, WIDE), 1) + kb * WIDE == own, 0.0, product)
            c[f, k * rows : (k + 1) * rows, here] = kept.astype(BF16)

    def make_out(kb):
        here = pl.ds(pl.multiple_of(kb * WIDE, WIDE), WIDE)
        for k in range(2):
            co[k * outs : (k + 1) * outs, here] = dot(yo[nfreq - 1, k], e[kb]).astype(BF16)

    def ring(steps_y, steps_z):
        return (group, ((my + steps_y) % SIDE) * SIDE + (mz + steps_z) % SIDE)

    def copy_block(f, ref, recv_sem, target):
        return pltpu.make_async_remote_copy(
            src_ref=ref, dst_ref=ref, send_sem=g_send.at[f], recv_sem=recv_sem,
            device_id=target, device_id_type=MESH,
        )

    def back(at, steps):
        return (at + SIDE - steps) % SIDE

    def first_leg(f, h, d):
        return copy_block(f, g.at[f, my, mz, h], first_recv.at[f, h, d - 1], ring(d, 0) if h == 0 else ring(0, d))

    def brought(f, h, d):
        return g.at[f, back(my, d), mz, h] if h == 0 else g.at[f, my, back(mz, d), h]

    def second_leg(f, h, d, far):
        return copy_block(f, brought(f, h, d), second_recv.at[f], ring(0, far) if h == 0 else ring(far, 0))

    def solve_and_share(f, sweep):
        wait_bytes(rbuf.at[f, 0 : devices - 1], a2a_recv.at[f])
        arrived = dot(unpack[...], rbuf[f].reshape(devices * SLOTS, 2 * loads))
        if sweep == 0:
            if f == 0:
                wait_bytes(drecv.at[0 : devices - 1], d_recv)
                both = jnp.abs(unpack[...].astype(F32)).astype(BF16)
                piv[...] = dot(both, drecv[...].reshape(devices * SLOTS, lane))
            gap[f] = arrived
            rest = arrived
        else:
            rest = gap[f] - arrived
        pr, pi = piv[:, 2 * f : 2 * f + 1], piv[:, 2 * f + 1 : 2 * f + 2]
        denom = pr * pr + pi * pi
        xr, xi = rest[:, :loads], rest[:, loads:]
        real = (pr * xr + pi * xi) / denom
        imag = (pr * xi - pi * xr) / denom
        if sweep == ITERS - 1:
            lam[f, 0] = real
            lam[f, 1] = imag
        g[f, my, mz] = jnp.concatenate([real, imag], axis=1).astype(BF16).reshape(2, cons // 2, 2 * loads)
        for d in NEAR_FIRST:
            for h in range(2):
                first_leg(f, h, d).start()
        for far in NEAR_FIRST:
            for h in range(2):
                second_leg(f, h, 0, far).start()

    def pass_on(f):
        for d in NEAR_FIRST:
            for h in range(2):
                first_leg(f, h, d).wait_recv()
                for far in NEAR_FIRST:
                    second_leg(f, h, d, far).start()

    def gathered(f):
        wait_bytes(g.at[f, 0:3], second_recv.at[f])
        return g[f].reshape(cons * devices, 2 * loads)

    def shared(f):
        wait_bytes(g.at[f, 0:3], g_send.at[f])
        wait_bytes(g.at[f, 0:3, 0:1], g_send.at[f])

    def complex_parts(products, count):
        top, low = products[:count], products[count:]
        return top[:, :loads] - low[:, loads:], top[:, loads:] + low[:, :loads]

    def multiply(f):
        real, imag = complex_parts(dot(c[f], gathered(f)), rows)
        shared(f)
        wait_bytes(sbuf.at[f, 0 : devices - 1], a2a_send.at[f])
        send_rows(f, jnp.concatenate([real, imag], axis=1))

    def correct(f, products):
        real, imag = complex_parts(products, outs)
        resp[f, 0] = resp[f, 0] - real
        resp[f, 1] = resp[f, 1] - imag

    def finish_spread(f):
        forces = gathered(f)
        size = 2 * WIDE

        def part(i, carry):
            here = pl.ds(pl.multiple_of(i * size, size), size)
            signs = jnp.concatenate([e[kb, here, :] for kb in range(blocks)], axis=1)
            spread[here, :] = dot(signs, forces).astype(BF16)
            return carry

        lax.fori_loop(0, width // size, part, 0)
        correct(f, dot(yo[f].reshape(2 * outs, width), spread[...]))
        shared(f)

    def finish_coupled(f):
        correct(f, dot(co[...], gathered(f)))
        shared(f)

    def span(fn, low, high):
        def one(i, carry):
            fn(i)
            return carry

        lax.fori_loop(low, high, one, 0)

    def signs_and_coupled(kb):
        make_signs(kb)
        make_coupled(0, kb)

    coupled_1 = functools.partial(make_coupled, 1)
    span(signs_and_coupled, 0, 2)
    solve_and_share(0, 0)
    span(signs_and_coupled, 2, 4)
    pass_on(0)
    span(signs_and_coupled, 4, 6)
    solve_and_share(1, 0)
    span(signs_and_coupled, 6, 8)
    multiply(0)
    pass_on(1)
    span(coupled_1, 0, C1[0])
    for f in range(nfreq):
        load_yo[f].wait()
    done = 0
    for sweep in range(1, ITERS):
        last = sweep == ITERS - 1
        solve_and_share(0, sweep)
        if sweep == 1:
            span(coupled_1, C1[0], C1[1])
            if C1[1] < blocks:
                pass_on(0)
                span(coupled_1, C1[1], blocks)
        multiply(1)
        if sweep > 1 or C1[1] == blocks:
            pass_on(0)
        if not last:
            span(make_out, done, done + OUT[sweep - 1][0])
            done += OUT[sweep - 1][0]
        solve_and_share(1, sweep)
        if last:
            pass_on(1)
            finish_spread(0)
        else:
            multiply(0)
            pass_on(1)
            for k in range(2):
                resp[sweep - 1, k] = dot(yo[sweep - 1, k], fo[...])
            span(make_out, done, done + OUT[sweep - 1][1])
            done += OUT[sweep - 1][1]
    finish_coupled(1)
    for f in range(nfreq):
        wait_bytes(sbuf.at[f, 0 : devices - 1], a2a_send.at[f])
    wait_bytes(dsend.at[0 : devices - 1], d_send)


def hand_over(resp, lam, resp_out, lam_out):
    resp_out[...] = resp[...]
    lam_out[...] = lam[...]


def on_device(y_inter, y_out, forces, pairs):
    nfreq, _, rows, width = y_inter.shape
    outs = y_out.shape[2]
    loads = forces.shape[1]
    devices = SIDE * SIDE
    cons = pairs.shape[0] // devices
    half = cons // 2
    dma = pltpu.SemaphoreType.DMA
    hbm = pl.BlockSpec(memory_space=pl.ANY)
    vmem = pl.BlockSpec(memory_space=pltpu.VMEM)
    made = pl.pallas_call(
        kernel,
        out_shape=(
            jax.ShapeDtypeStruct((nfreq, 2, outs, loads), F32),
            jax.ShapeDtypeStruct((nfreq, 2, cons, loads), F32),
        ),
        in_specs=[hbm, hbm, hbm, vmem],
        out_specs=(vmem, vmem),
        scratch_shapes=[
            pltpu.VMEM(y_inter.shape, BF16),
            pltpu.VMEM(y_out.shape, BF16),
            pltpu.VMEM(forces.shape, BF16),
            pltpu.VMEM((pairs.shape[0] // WIDE, width, WIDE), BF16),
            pltpu.VMEM((nfreq, 2 * rows, pairs.shape[0]), BF16),
            pltpu.VMEM((2 * outs, pairs.shape[0]), BF16),
            pltpu.VMEM((width, 2 * loads), BF16),
            pltpu.VMEM((nfreq, SIDE, SIDE, 2, half, 2 * loads), BF16),
            pltpu.VMEM((nfreq, devices, SLOTS, 2 * loads), BF16),
            pltpu.VMEM((nfreq, devices, SLOTS, 2 * loads), BF16),
            pltpu.VMEM((devices, SLOTS, 128), BF16),
            pltpu.VMEM((devices, SLOTS, 128), BF16),
            pltpu.VMEM((nfreq, cons, 2 * loads), F32),
            pltpu.VMEM((cons, 128), F32),
            pltpu.VMEM((devices * SLOTS, rows), BF16),
            pltpu.VMEM((cons, devices * SLOTS), BF16),
            pltpu.VMEM((rows, 1), jnp.int32),
            pltpu.VMEM((rows, 1), jnp.int32),
            pltpu.VMEM((rows, 128), BF16),
            dma((1 + 2 * nfreq + nfreq,)),
            dma((nfreq,)),
            dma((nfreq,)),
            dma,
            dma,
            dma((nfreq,)),
            dma((nfreq, 2, SIDE - 1)),
            dma((nfreq,)),
        ],
        compiler_params=pltpu.CompilerParams(collective_id=0, has_side_effects=True, vmem_limit_bytes=60 * 2**20),
    )(y_inter, y_out, forces, pairs.T)
    return pl.pallas_call(
        hand_over,
        out_shape=tuple(jax.ShapeDtypeStruct(m.shape, F32) for m in made),
        in_specs=[vmem, vmem],
        out_specs=(vmem, vmem),
    )(*made)


def solution(mesh):
    placed = P("freq", None, "rows", None)
    return jax.shard_map(
        on_device,
        mesh=mesh,
        in_specs=(placed, placed, P(), P()),
        out_specs=(placed, placed),
        check_vma=False,
    )
```
